32 devices in a mesh: seq: 4 (over y, x), fsdp: 8 (over z, core).
Axes of the slice: x: 2, y: 2, z: 4, core: 2. Of those that a mesh axis runs over, the one named last changes fastest.
Arguments:
- byte_rows: bfloat16 [8, 4096, 512], P('fsdp', 'seq'), may hold values from -6 to 6
- cotangent: bfloat16 [8, 4096, 512], P('fsdp', 'seq'), may hold values from -6 to 6
- doc_ids: int32 [8, 4096], P('fsdp', 'seq'), may hold values from 0 to 7, never falling along the last dimension, each value on 1 to 2048 neighbouring positions
- conv_weight: bfloat16 [8, 32, 16, 16], replicated, may hold values from -0.5 to 0.5
- norm_gain: float32 [512], replicated, may hold values from 0.5 to 1.5
- proj_weight: bfloat16 [4096, 512], P('fsdp'), may hold values from -0.25 to 0.25
- round_seed: int32 [1], replicated, may hold values from 0 to 1073741823
- step_count: int32 [1], replicated, may hold values from 0 to 999999
Outputs:
- grad_bytes: float32 [8, 4096, 512], P('fsdp', 'seq')
- grad_proj: float32 [4096, 512], P('fsdp')
- grad_conv: float32 [8, 32, 16, 16], replicated
- grad_gain: float32 [512], replicated
The draws below stay inside these ranges and needn't reach their ends.
Inputs may be any that keep to these rules, and one draw needn't show every extreme that they name: `doc_ids`: along each sequence the document numbers never fall; no document covers more than 2048 bytes, and one covers exactly 2048.
All inputs are finite; a program needn't handle non-finite values.
Results may differ from the reference program's by a relative error of at most 0.0046.
Values may be sent and summed in bfloat16 or wider, within the bound.
A program may use at most 128 MiB of HBM per device.

```python
import math
import jax
import jax.numpy as jnp
import numpy as np
from jax import lax

D = 512
GROUPS = 32
KERNEL = 8
STRIDE = 4
CG = 16
FF = 4096
LEN = 4096
SEQS = 8
DOCS = 8
DOC_MOST = 2048


def levels(stream_key, shape, shards, low, largest):
    gain = 1.0
    for axis_at, shards_of in shards:
        draws = jax.random.uniform(jax.random.fold_in(jax.random.fold_in(stream_key, 6), axis_at), (shards_of,), jnp.float32, low / len(shards), largest / len(shards))
        gain = gain * jnp.repeat(jnp.exp(draws), shape[axis_at] // shards_of).reshape((-1,) + (1,) * (len(shape) - 1 - axis_at))
    return gain


def length_profile(count, total, reach, skew):
    weights = [(1 << 20) // math.isqrt(rank ** skew) + 1 for rank in range(2, count + 1)]
    rest, counts = total - reach - (count - 1), [1] * (count - 1)
    while rest > 0:
        movable = [i for i in range(count - 1) if counts[i] < reach]
        mass, left = sum([weights[i] for i in movable]), rest
        for i in movable:
            extra = min(reach - counts[i], max(1, left * weights[i] // mass), rest)
            counts[i] = counts[i] + extra
            rest = rest - extra
    return np.array([reach] + counts)


def uneven_parts(stream_key, amount, total, bound, slope):
    if amount == 2:
        one = jax.random.randint(stream_key, (), max(1, total - bound), min(bound, total - 1) + 1)
        return jnp.stack([one, total - one])
    sizes = jnp.asarray(length_profile(amount, total, bound, slope), jnp.int32)
    couples = (amount - 1) // 2
    giver, receiver = sizes[1:1 + 2 * couples:2], sizes[2:2 + 2 * couples:2]
    slack = jnp.minimum(giver - 1, bound - receiver)
    passed = jax.random.randint(jax.random.fold_in(stream_key, 1), (couples,), 0, 1 << 20) % (slack + 1)
    sizes = sizes.at[1:1 + 2 * couples:2].set(giver - passed).at[2:2 + 2 * couples:2].set(receiver + passed)
    return sizes[jax.random.permutation(jax.random.fold_in(stream_key, 2), amount)]


def bell_draw(rng, shape, width, reach, pieces=(), kind=jnp.bfloat16):
    result = jax.random.normal(rng, shape, jnp.float32) * width
    if len(pieces) > 0:
        result = levels(rng, shape, pieces, -0.22, 0.18) * result
    return jnp.clip(result, min=-reach, max=reach).astype(kind)


def setup_inputs(seed: int = 0) -> dict:
    streams_of = jax.random.split(jax.random.key(seed), 9)
    return {
        "byte_rows": bell_draw(streams_of[0], (SEQS, LEN, D), 1.0, 6.0, ((0, 8), (1, 4))),
        "cotangent": bell_draw(streams_of[1], (SEQS, LEN, D), 1.0, 6.0, ((0, 8), (1, 4))),
        "doc_ids": jax.vmap(lambda own: jnp.searchsorted(jnp.cumsum(uneven_parts(own, DOCS, LEN, DOC_MOST, 2)), jnp.arange(LEN), side="right"))(jax.random.split(streams_of[2], SEQS)).reshape((SEQS, LEN)).astype(jnp.int32),
        "conv_weight": bell_draw(streams_of[3], (KERNEL, GROUPS, CG, CG), (KERNEL * CG) ** -0.5, 0.5),
        "norm_gain": jnp.clip(1.0 + 0.1 * jax.random.normal(streams_of[4], (D,), jnp.float32), 0.5, 1.5),
        "proj_weight": bell_draw(streams_of[5], (FF, D), D ** -0.5, 0.25, ((0, 8),)),
        "round_seed": jax.random.randint(streams_of[6], (1,), 0, 1073741824).astype(jnp.int32),
        "step_count": jax.random.randint(streams_of[7], (1,), 0, 1000000).astype(jnp.int32),
    }


GELU_A = 0.7978845608028654
GELU_B = 0.044715
QUANT = 0.25

def gelu_grad(values):
    tangent = jnp.tanh(GELU_A * (values + GELU_B * values * values * values))
    return 0.5 * (1.0 + tangent) + 0.5 * values * (1.0 - tangent * tangent) * GELU_A * (1.0 + 3.0 * GELU_B * values * values)

def mix_bits(flat_index, seed_value, step_value):
    hashed = flat_index * jnp.int32(-1640531535) + seed_value * jnp.int32(-2048144777) + step_value * jnp.int32(-1028477379)
    hashed = hashed ^ lax.shift_right_logical(hashed, jnp.int32(16))
    hashed = hashed * jnp.int32(2146121005)
    hashed = hashed ^ lax.shift_right_logical(hashed, jnp.int32(15))
    hashed = hashed * jnp.int32(-2073254261)
    hashed = hashed ^ lax.shift_right_logical(hashed, jnp.int32(16))
    return lax.shift_right_logical(hashed, jnp.int32(8)).astype(jnp.float32) / 16777216.0

def tap_windows(series, extra_rows, patches):
    joined = jnp.concatenate([series, extra_rows], 0)
    tail_shape = joined.shape[1:]
    lower = joined[:-STRIDE].reshape((patches, STRIDE) + tail_shape)
    upper = joined[STRIDE:].reshape((patches, STRIDE) + tail_shape)
    return jnp.concatenate([lower, upper], 1)

def one_sequence(byte_block, upstream, doc_block, conv_weight, norm_gain, proj_weight):
    length = byte_block.shape[0]
    patches = length // STRIDE
    pad_rows = jnp.zeros((STRIDE, D), jnp.bfloat16)
    pad_docs = jnp.zeros((STRIDE,), jnp.int32)
    window = tap_windows(byte_block, pad_rows, patches)
    up_window = tap_windows(upstream, pad_rows, patches)
    doc_window = tap_windows(doc_block, pad_docs, patches)
    position = STRIDE * jnp.arange(patches, dtype=jnp.int32)[:, None] + jnp.arange(KERNEL, dtype=jnp.int32)[None, :]
    keep_tap = (doc_window == doc_window[:, :1]) & (position < length)
    keep_f = keep_tap.astype(jnp.float32)[:, :, None]
    masked = (window.astype(jnp.float32) * keep_f).astype(jnp.bfloat16)
    grouped = masked.reshape(patches, KERNEL, GROUPS, CG).astype(jnp.float32)
    conv_f = conv_weight.astype(jnp.float32)
    hidden = jnp.einsum('pkgc,kgcd->pgd', grouped, conv_f).reshape(patches, D)
    factor = lax.rsqrt(lax.optimization_barrier(jnp.mean(hidden * hidden, axis=-1, keepdims=True)) + 1e-06)
    normed = (hidden * factor * norm_gain).astype(jnp.bfloat16)
    pre_act = jnp.dot(normed, proj_weight.T, preferred_element_type=jnp.float32)
    grad_pre = up_window.astype(jnp.float32) * keep_f * gelu_grad(pre_act.reshape(patches, KERNEL, D))
    grad_pre = grad_pre.reshape(patches, FF).astype(jnp.bfloat16)
    grad_norm = jnp.dot(grad_pre, proj_weight, preferred_element_type=jnp.float32)
    proj_part = jnp.dot(grad_pre.T, normed, preferred_element_type=jnp.float32)
    gain_part = lax.optimization_barrier(jnp.sum(grad_norm * hidden * factor, axis=0))
    gained = norm_gain * grad_norm
    grad_hidden = factor * gained - hidden * factor * factor * factor * lax.optimization_barrier(jnp.mean(gained * hidden, axis=-1, keepdims=True))
    grad_hidden = grad_hidden.reshape(patches, GROUPS, CG)
    conv_part = jnp.einsum('pkgc,pgd->kgcd', grouped, grad_hidden, precision=lax.Precision.HIGHEST)
    grad_window = jnp.einsum('pgd,kgcd->pkgc', grad_hidden, conv_f, precision=lax.Precision.HIGHEST)
    grad_window = grad_window.reshape(patches, KERNEL, D) * keep_f
    back_rows = jnp.zeros((length + STRIDE, D), jnp.float32)
    back_rows = back_rows.at[:length].add(grad_window[:, :STRIDE].reshape(length, D))
    back_rows = back_rows.at[STRIDE:].add(grad_window[:, STRIDE:].reshape(length, D))
    grad_rows = upstream.astype(jnp.float32) + back_rows[:length]
    return (grad_rows, proj_part, gain_part, conv_part)

def reference(byte_rows, cotangent, doc_ids, conv_weight, norm_gain, proj_weight, round_seed, step_count):

    def visit(carry, inputs):
        grad_rows, proj_part, gain_part, conv_part = one_sequence(inputs[0], inputs[1], inputs[2], conv_weight, norm_gain, proj_weight)
        return ((carry[0] + proj_part, carry[1] + gain_part, carry[2] + conv_part), grad_rows)
    start_carry = (jnp.zeros((FF, D), jnp.float32), jnp.zeros((D,), jnp.float32), jnp.zeros((KERNEL, GROUPS, CG, CG), jnp.float32))
    sums, grad_bytes = lax.scan(visit, start_carry, (byte_rows, cotangent, doc_ids))
    grad_scale = 1.0 / math.sqrt(SEQS * LEN // STRIDE)
    flat_index = jnp.arange(FF, dtype=jnp.int32)[:, None] * jnp.int32(D) + jnp.arange(D, dtype=jnp.int32)[None, :]
    dither_noise = mix_bits(flat_index, round_seed[0], step_count[0])
    grad_proj = sums[0] * grad_scale + QUANT * (dither_noise - 0.5)
    return (grad_bytes, grad_proj, sums[2] * grad_scale, sums[1] * grad_scale)
```

```python
import functools
import math

import jax
import jax.numpy as jnp
from jax import lax
from jax.experimental import pallas as pl
from jax.experimental.pallas import tpu as pltpu
from jax.sharding import PartitionSpec as P

GROUPS = 32
KERNEL = 8
STRIDE = 4
CG = 16
D = GROUPS * CG

GELU_A = 0.7978845608028654
GELU_B = 0.044715
QUANT = 0.25

MESH = pl.DeviceIdType.MESH
BF = jnp.bfloat16
F32 = jnp.float32


def gelu_grad(values):
    tangent = jnp.tanh(GELU_A * (values + GELU_B * values * values * values))
    return 0.5 * (1.0 + tangent) + 0.5 * values * (1.0 - tangent * tangent) * GELU_A * (
        1.0 + 3.0 * GELU_B * values * values
    )


def mix_bits(flat_index, seed_value, step_value):
    hashed = (
        flat_index * jnp.int32(-1640531535)
        + seed_value * jnp.int32(-2048144777)
        + step_value * jnp.int32(-1028477379)
    )
    hashed = hashed ^ lax.shift_right_logical(hashed, jnp.int32(16))
    hashed = hashed * jnp.int32(2146121005)
    hashed = hashed ^ lax.shift_right_logical(hashed, jnp.int32(15))
    hashed = hashed * jnp.int32(-2073254261)
    hashed = hashed ^ lax.shift_right_logical(hashed, jnp.int32(16))
    return lax.shift_right_logical(hashed, jnp.int32(8)).astype(F32) / 16777216.0


def dot(a, b, ca, cb):
    return lax.dot_general(a, b, (((ca,), (cb,)), ((), ())), preferred_element_type=F32)


def wide(mask):
    return jnp.concatenate([mask] * (D // 128), axis=1)


def kernel(
    n_s, n_z, scale,
    x_ref, ct_ref, doc_ref, cw_ref, gain_ref, pw_ref, seed_ref, step_ref,
    gb_ref, gpo_ref, co_ref,
    xf, cf, df, hx, hc, hd, win, up, kp, wd, w, gpo, gps, ps, rs1, sf, own, rs2, zs, fin, dith,
    gn, hid, fac, norm, gh, hsend, hrecv,
    pacc, cp, cpx, c1, c2, c3, c4, c5,
    sem_l, sem_h, s1, r1, s2, r2, s3, r3, sg, rg, sn, ss, rs, sz, rz, sf_s, sf_r, sc, rc,
):
    s = lax.axis_index("seq")
    f = lax.axis_index("fsdp")
    z = f // 2
    c = f % 2
    length = ct_ref.shape[0]
    patches = length // STRIDE
    pr = pw_ref.shape[0]
    q = pr // n_s
    parts = D // pr
    half_rows = (D // 2) // n_s

    def copy(src, dst, send, recv, dev):
        cpy = pltpu.make_async_remote_copy(
            src_ref=src, dst_ref=dst, send_sem=send, recv_sem=recv, device_id=dev, device_id_type=MESH
        )
        cpy.start()

    def drain(ref, sem):
        pltpu.make_async_copy(ref, ref, sem).wait()

    partner = (s, 2 * z + 1 - c)
    mypart = pl.ds(pl.multiple_of(c * patches, patches), patches)

    def zdev(i):
        zi = lax.rem(z + i, n_z)
        return zi, (s, 2 * zi + c)

    def sdev(i):
        si = lax.rem(s + i, n_s)
        return si, (si, f)

    own_panel = pltpu.make_async_copy(pw_ref, w.at[f], sem_l.at[0])
    own_panel.start()

    barrier = pltpu.get_barrier_semaphore()
    pl.semaphore_signal(barrier, inc=1, device_id=partner, device_id_type=MESH)
    for i in range(1, n_z):
        pl.semaphore_signal(barrier, inc=1, device_id=zdev(i)[1], device_id_type=MESH)
    for i in range(1, n_s):
        pl.semaphore_signal(barrier, inc=1, device_id=sdev(i)[1], device_id_type=MESH)
    pl.semaphore_wait(barrier, 1 + (n_z - 1) + (n_s - 1))

    for i in range(1, n_z):
        _, dev = zdev(n_z - i)
        copy(pw_ref.at[pl.ds(pl.multiple_of(s * q, q), q)],
             w.at[f, pl.ds(pl.multiple_of(s * q, q), q)], s1.at[i], r1.at[z], dev)
    copy(pw_ref, w.at[f], s3.at[z], r3.at[z], partner)

    @pl.when(s > 0)
    def _():
        dev = (s - 1, f)
        copy(x_ref.at[pl.ds(0, 16)], hx, sem_h.at[0], sem_h.at[1], dev)
        copy(ct_ref.at[pl.ds(0, 16)], hc, sem_h.at[2], sem_h.at[3], dev)
        copy(doc_ref.at[:, pl.ds(0, 128)], hd, sem_h.at[4], sem_h.at[5], dev)

    for lb in range(4):
        xf[lb, pl.ds(0, length)] = x_ref[:, lb * 128:(lb + 1) * 128].astype(F32)
        cf[lb, pl.ds(0, length)] = ct_ref[:, lb * 128:(lb + 1) * 128].astype(F32)
    df[pl.ds(0, length)] = jnp.transpose(
        jnp.broadcast_to(doc_ref[...].astype(F32), (128, length)), (1, 0)
    )

    spread = (
        lax.broadcasted_iota(jnp.int32, (CG, 256), 1) % CG
        == lax.broadcasted_iota(jnp.int32, (CG, 256), 0)
    ).astype(F32).astype(BF)
    diag = (
        lax.broadcasted_iota(jnp.int32, (256, 256), 0) // CG
        == lax.broadcasted_iota(jnp.int32, (256, 256), 1) // CG
    )

    def build(kb, carry):
        piece = cw_ref[pl.ds(pl.multiple_of(kb * 256, 256), 256), :]
        wd[kb] = jnp.where(diag, dot(piece, spread, 1, 0), 0.0).astype(BF)
        return carry

    lax.fori_loop(0, 2 * KERNEL, build, 0)

    @pl.when(s == n_s - 1)
    def _():
        xf[:, pl.ds(length, 8)] = jnp.zeros((4, 8, 128), F32)
        cf[:, pl.ds(length, 8)] = jnp.zeros((4, 8, 128), F32)
        df[pl.ds(length, 8)] = jnp.full((8, 128), -1.0, F32)

    @pl.when(s < n_s - 1)
    def _():
        drain(hx, sem_h.at[1])
        drain(hc, sem_h.at[3])
        drain(hd, sem_h.at[5])
        top = hx[...].astype(F32)
        topc = hc[...].astype(F32)
        for lb in range(4):
            xf[lb, pl.ds(length, 8)] = top[:8, lb * 128:(lb + 1) * 128]
            cf[lb, pl.ds(length, 8)] = topc[:8, lb * 128:(lb + 1) * 128]
        df[pl.ds(length, 8)] = jnp.transpose(
            jnp.broadcast_to(hd[...].astype(F32), (128, 128)), (1, 0)
        )[:8]

    @pl.when(s > 0)
    def _():
        drain(hx, sem_h.at[0])
        drain(hc, sem_h.at[2])
        drain(hd, sem_h.at[4])

    def taps(ref, k):
        return jnp.concatenate(
            [ref[lb, pl.ds(k, patches, stride=STRIDE), :] for lb in range(4)], axis=1
        )

    first_doc = df[pl.ds(0, patches, stride=STRIDE), :]
    for k in range(KERNEL):
        keep = (df[pl.ds(k, patches, stride=STRIDE), :] == first_doc).astype(F32)
        kp[k] = keep
        kw = wide(keep)
        win[k] = (taps(xf, k) * kw).astype(BF)
        upk = (taps(cf, k) * kw).astype(BF)
        for part in range(parts):
            up[k * parts + part] = upk[:, part * pr:(part + 1) * pr]

    def forward(i, carry):
        zi = lax.rem(z + i, n_z)
        fi = 2 * zi + c
        piece = w.at[fi, pl.ds(pl.multiple_of(s * q, q), q)]
        drain(piece, r1.at[zi])
        for j in range(1, n_s):
            _, dev = sdev(j)
            copy(piece, piece, s2.at[zi], r2.at[zi], dev)
        return carry

    lax.fori_loop(1, n_z, forward, 0)

    hid[...] = jnp.zeros_like(hid)

    def conv(k, carry):
        for b in range(2):
            hid[:, b * 256:(b + 1) * 256] += dot(win[k, :, b * 256:(b + 1) * 256], wd[2 * k + b], 1, 0)
        return carry

    lax.fori_loop(0, KERNEL, conv, 0)
    hidden = hid[...]
    factor = lax.rsqrt(jnp.mean(hidden * hidden, axis=-1, keepdims=True) + 1e-06)
    fac[...] = jnp.broadcast_to(factor, (patches, 128))
    norm[mypart] = (hidden * factor * gain_ref[...]).astype(BF)
    copy(norm.at[mypart], norm.at[mypart], sn.at[0], sn.at[1], partner)
    gn[...] = jnp.zeros_like(gn)
    own_panel.wait()

    def panel(fi, dst):
        pre = dot(norm[mypart], w[fi], 1, 1)
        g = (up[fi].astype(F32) * gelu_grad(pre)).astype(BF)
        dst[...] = g
        gn[...] += dot(g, w[fi], 1, 0)

    def sums(zi):
        drain(gps.at[0], rg.at[zi])
        total = dot(gpo[zi], norm[...], 0, 0)
        sf[...] = total
        ps[zi] = total.astype(BF)
        own[zi] = sf[pl.ds(pl.multiple_of(s * q, q), q), :]
        for j in range(1, n_s):
            sj, dev = sdev(j)
            copy(ps.at[zi, pl.ds(pl.multiple_of(sj * q, q), q)], rs1.at[zi, s], ss.at[zi], rs.at[zi], dev)

    def step(i, carry):
        zi = lax.rem(z + i, n_z)

        @pl.when(i > 0)
        def _():
            drain(w.at[0, pl.ds(0, (n_s - 1) * q)], r2.at[zi])
            copy(w.at[2 * zi + c], w.at[2 * zi + c], s3.at[zi], r3.at[zi], partner)

        panel(2 * zi + c, gpo.at[zi, mypart])
        drain(w.at[0], r3.at[zi])
        panel(2 * zi + 1 - c, gps.at[zi])
        copy(gps.at[zi], gpo.at[zi, mypart], sg.at[zi], rg.at[zi], partner)

        @pl.when(i == 0)
        def _():
            drain(gh, sn.at[1])

        @pl.when(i > 0)
        def _():
            sums(lax.rem(z + i - 1, n_z))

        return carry

    lax.fori_loop(0, n_z, step, 0)
    sums(lax.rem(z + n_z - 1, n_z))

    hidden = hid[...]
    factor = fac[:, :1]
    grad_norm = gn[...]
    gain_part = jnp.sum(grad_norm * hidden * factor, axis=0, keepdims=True)
    gained = gain_ref[...] * grad_norm
    gh[...] = (
        factor * gained
        - hidden * (factor * factor * factor) * jnp.mean(gained * hidden, axis=-1, keepdims=True)
    ).astype(BF)

    def upper(t):
        return wide(kp[STRIDE + t]) * jnp.concatenate(
            [dot(gh[:, b * 256:(b + 1) * 256], wd[2 * (STRIDE + t) + b], 1, 1) for b in range(2)], axis=1
        )

    cols = lax.broadcasted_iota(jnp.int32, (128, 128), 1) // CG
    small = lax.broadcasted_iota(jnp.int32, (128, 128), 0) // CG == cols
    pacc[...] = jnp.zeros_like(pacc)

    def conv_back(k, carry):
        for b in range(4):
            lanes = slice(b * 128, (b + 1) * 128)
            full = jnp.where(small, dot(jnp.transpose(win[k, :, lanes], (1, 0)), gh[:, lanes], 1, 0), 0.0)
            full = full + pltpu.roll(full, 64, 1)
            full = full + pltpu.roll(full, 32, 1)
            full = full + pltpu.roll(full, 16, 1)
            pacc[lanes, :] = jnp.where(cols == k, full, pacc[lanes, :])
        return carry

    [conv_back(k, 0) for k in range(KERNEL)]
    cp[...] = jnp.zeros_like(cp)
    cp[:, :, pl.ds(0, half_rows), :] = pacc[...].reshape(2, n_s, half_rows, 128)
    for b in range(4):
        cp[0, 0, pl.ds(half_rows + b, 1), :] = gain_part[:, b * 128:(b + 1) * 128]
    copy(cp.at[1 - c], cpx, sc.at[0], rc.at[0], partner)

    def reduce_seq(i, carry):
        zi = lax.rem(z + i, n_z)
        drain(rs1.at[0, pl.ds(0, n_s - 1)], rs.at[zi])
        total = own[zi]
        for j in range(1, n_s):
            total = total + rs1[zi, sdev(j)[0]].astype(F32)

        @pl.when(i > 0)
        def _():
            zs[i] = total.astype(BF)
            copy(zs.at[i], rs2.at[z], sz.at[i], rz.at[i], (s, 2 * zi + c))

        @pl.when(i == 0)
        def _():
            own[z] = total

        return carry

    lax.fori_loop(0, n_z - 1, reduce_seq, 0)

    drain(cpx, rc.at[0])
    c1[...] = cp[c] + cpx[...]
    for j in range(1, n_s):
        sj, dev = sdev(j)
        copy(c1.at[sj], c2.at[s], sc.at[1], rc.at[1], dev)

    row = lax.broadcasted_iota(jnp.int32, (patches, D), 0)
    for t in range(STRIDE):
        hi = upper(t)
        hsend[pl.ds(t, 1), :] = hi[patches - 1:, :]
        lo = wide(kp[t]) * jnp.concatenate(
            [dot(gh[:, b * 256:(b + 1) * 256], wd[2 * t + b], 1, 1) for b in range(2)], axis=1
        )
        value = taps(cf, t) + lo + jnp.where(row == 0, 0.0, pltpu.roll(hi, 1, 0))
        for lb in range(4):
            xf[lb, pl.ds(t, patches, stride=STRIDE), :] = value[:, lb * 128:(lb + 1) * 128]

    @pl.when(s < n_s - 1)
    def _():
        copy(hsend, hrecv, sem_h.at[6], sem_h.at[7], (s + 1, f))

    lax.fori_loop(n_z - 1, n_z, reduce_seq, 0)

    drain(c2.at[pl.ds(0, n_s - 1)], rc.at[1])
    total = c1[s]
    for j in range(1, n_s):
        total = total + c2[sdev(j)[0]]
    c3[z] = total
    for i in range(1, n_z):
        copy(c3.at[z], c3.at[z], sc.at[2], rc.at[2], zdev(i)[1])

    for lb in range(4):
        gb_ref[:, lb * 128:(lb + 1) * 128] = xf[lb, pl.ds(0, length)]

    shape = (pr, D)
    flat = (f * pr + lax.broadcasted_iota(jnp.int32, shape, 0)) * jnp.int32(D) + lax.broadcasted_iota(
        jnp.int32, shape, 1
    )
    dith[...] = QUANT * (mix_bits(flat, seed_ref[0], step_ref[0]) - 0.5)

    drain(c3.at[pl.ds(0, n_z - 1)], rc.at[2])
    total = c3[0]
    for i in range(1, n_z):
        total = total + c3[i]
    c4[s] = total
    for j in range(1, n_s):
        copy(c4.at[s], c4.at[s], sc.at[3], rc.at[3], sdev(j)[1])

    total = own[z]
    for i in range(1, n_z):
        drain(rs2.at[0], rz.at[i])
        total = total + rs2[zdev(n_z - i)[0]].astype(F32)
    mine = pl.ds(pl.multiple_of(s * q, q), q)
    fin[mine] = total.astype(BF)
    for j in range(1, n_s):
        copy(fin.at[mine], fin.at[mine], sf_s.at[0], sf_r.at[0], sdev(j)[1])

    drain(c4.at[pl.ds(0, n_s - 1)], rc.at[3])
    copy(c4, c5, sc.at[4], rc.at[4], partner)

    @pl.when(s > 0)
    def _():
        drain(hrecv, sem_h.at[7])
        gb_ref[pl.ds(0, 8), :] += jnp.where(
            lax.broadcasted_iota(jnp.int32, (8, D), 0) < STRIDE, hrecv[...], 0.0
        )

    @pl.when(s < n_s - 1)
    def _():
        drain(hsend, sem_h.at[6])

    co_ref[c] = c4[...] * scale
    drain(c5, rc.at[4])
    co_ref[1 - c] = c5[...] * scale

    drain(fin.at[pl.ds(0, (n_s - 1) * q)], sf_r.at[0])
    gpo_ref[...] = fin[...].astype(F32) * scale + dith[...]

    for i in range(1, n_z):
        drain(w.at[0, pl.ds(0, q)], s1.at[i])
        drain(zs.at[0], sz.at[i])
        zi, _ = zdev(i)
        drain(w.at[0, pl.ds(0, (n_s - 1) * q)], s2.at[zi])
    for i in range(n_z):
        drain(w.at[0], s3.at[i])
        drain(gps.at[0], sg.at[i])
        drain(rs1.at[0, pl.ds(0, n_s - 1)], ss.at[i])
    drain(gh, sn.at[0])
    drain(cpx, sc.at[0])
    drain(c2.at[pl.ds(0, n_s - 1)], sc.at[1])
    drain(c3.at[pl.ds(0, n_z - 1)], sc.at[2])
    drain(c4.at[pl.ds(0, n_s - 1)], sc.at[3])
    drain(c4, sc.at[4])
    drain(fin.at[pl.ds(0, (n_s - 1) * q)], sf_s.at[0])


def per_device(
    n_s, n_f, byte_rows, cotangent, doc_ids, conv_weight, norm_gain, proj_weight, round_seed, step_count
):
    length = byte_rows.shape[1]
    patches = length // STRIDE
    pr = proj_weight.shape[0]
    n_z = n_f // 2
    q = pr // n_s
    rows = (D // 2) // n_s + 8
    scale = 1.0 / math.sqrt(patches * n_s * n_f)
    v = pltpu.VMEM
    dma = pltpu.SemaphoreType.DMA
    vm = pl.BlockSpec(memory_space=pltpu.VMEM)
    smem = pl.BlockSpec(memory_space=pltpu.SMEM)
    scratch = [
        v((4, length + 8, 128), F32), v((4, length + 8, 128), F32), v((length + 8, 128), F32),
        v((16, D), BF), v((16, D), BF), v((1, 128), jnp.int32),
        v((KERNEL, patches, D), BF), v((n_f, patches, pr), BF), v((KERNEL, patches, 128), F32),
        v((2 * KERNEL, 256, 256), BF), v((n_f, pr, D), BF),
        v((n_z, 2 * patches, pr), BF), v((n_z, patches, pr), BF),
        v((n_z, pr, D), BF), v((n_z, n_s, q, D), BF), v((pr, D), F32), v((n_z, q, D), F32),
        v((n_z, q, D), BF), v((n_z, q, D), BF), v((pr, D), BF), v((pr, D), F32),
        v((patches, D), F32), v((patches, D), F32), v((patches, 128), F32),
        v((2 * patches, D), BF), v((patches, D), BF),
        v((8, D), F32), v((8, D), F32),
        v((D, 128), F32), v((2, n_s, rows, 128), F32), v((n_s, rows, 128), F32),
        v((n_s, rows, 128), F32), v((n_s, rows, 128), F32), v((n_z, rows, 128), F32),
        v((n_s, rows, 128), F32), v((n_s, rows, 128), F32),
        dma((1,)), dma((8,)), dma((n_z,)), dma((n_z,)), dma((n_z,)), dma((n_z,)), dma((n_z,)), dma((n_z,)),
        dma((n_z,)), dma((n_z,)), dma((2,)), dma((n_z,)), dma((n_z,)), dma((n_z,)), dma((n_z,)),
        dma((1,)), dma((1,)), dma((5,)), dma((5,)),
    ]
    grad_bytes, grad_proj, packed = pl.pallas_call(
        functools.partial(kernel, n_s, n_z, scale),
        out_shape=(
            jax.ShapeDtypeStruct((length, D), F32),
            jax.ShapeDtypeStruct((pr, D), F32),
            jax.ShapeDtypeStruct((2, n_s, rows, 128), F32),
        ),
        in_specs=[vm, vm, vm, vm, vm, pl.BlockSpec(memory_space=pl.ANY), smem, smem],
        out_specs=(vm, vm, vm),
        scratch_shapes=scratch,
        compiler_params=pltpu.CompilerParams(
            collective_id=0, has_side_effects=True, vmem_limit_bytes=58 * 1024 * 1024
        ),
    )(
        byte_rows[0], cotangent[0], doc_ids, conv_weight.reshape(KERNEL * D, CG), norm_gain[None],
        proj_weight, round_seed, step_count,
    )
    grad_gain = packed[0, 0, rows - 8 : rows - 4].reshape(D)
    grad_conv = packed[:, :, : rows - 8].reshape(GROUPS, CG, KERNEL, CG).transpose(2, 0, 1, 3)
    return grad_bytes[None], grad_proj, grad_conv, grad_gain


def solution(mesh):
    in_specs = (
        P("fsdp", "seq", None),
        P("fsdp", "seq", None),
        P("fsdp", "seq"),
        P(),
        P(),
        P("fsdp", None),
        P(),
        P(),
    )
    out_specs = (P("fsdp", "seq", None), P("fsdp", None), P(), P())
    return jax.shard_map(
        functools.partial(per_device, mesh.shape["seq"], mesh.shape["fsdp"]),
        mesh=mesh, in_specs=in_specs, out_specs=out_specs, check_vma=False,
    )
```

```python
import functools
import math

import jax
import jax.numpy as jnp
from jax import lax
from jax.experimental import pallas as pl
from jax.experimental.pallas import tpu as pltpu
from jax.sharding import PartitionSpec as P

GROUPS = 32
KERNEL = 8
STRIDE = 4
CG = 16
D = GROUPS * CG

GELU_A = 0.7978845608028654
GELU_B = 0.044715
QUANT = 0.25

MESH = pl.DeviceIdType.MESH
BF = jnp.bfloat16
F32 = jnp.float32


def gelu_grad(values):
    tangent = jnp.tanh(GELU_A * (values + GELU_B * values * values * values))
    return 0.5 * (1.0 + tangent) + 0.5 * values * (1.0 - tangent * tangent) * GELU_A * (
        1.0 + 3.0 * GELU_B * values * values
    )


def mix_bits(flat_index, seed_value, step_value):
    hashed = (
        flat_index * jnp.int32(-1640531535)
        + seed_value * jnp.int32(-2048144777)
        + step_value * jnp.int32(-1028477379)
    )
    hashed = hashed ^ lax.shift_right_logical(hashed, jnp.int32(16))
    hashed = hashed * jnp.int32(2146121005)
    hashed = hashed ^ lax.shift_right_logical(hashed, jnp.int32(15))
    hashed = hashed * jnp.int32(-2073254261)
    hashed = hashed ^ lax.shift_right_logical(hashed, jnp.int32(16))
    return lax.shift_right_logical(hashed, jnp.int32(8)).astype(F32) / 16777216.0


def dot(a, b, ca, cb):
    return lax.dot_general(a, b, (((ca,), (cb,)), ((), ())), preferred_element_type=F32)


def wide(mask):
    return jnp.concatenate([mask] * (D // 128), axis=1)


def kernel(
    n_s, n_z, scale,
    x_ref, ct_ref, doc_ref, cw_ref, gain_ref, pw_ref, seed_ref, step_ref,
    gb_ref, gpo_ref, conv_ref, go_ref,
    co_ref, xf, cf, df, hx, hc, hd, win, up, kp, wd, w, gpo, gps, ps, rs1, sf, own, rs2, zs, fin, dith,
    gn, hid, fac, norm, gh, hsend, hrecv,
    pacc, cp, cpx, c1, c2, c3, c4, c5,
    sem_l, sem_h, s1, r1, s2, r2, s3, r3, sg, rg, sn, ss, rs, sz, rz, sf_s, sf_r, sc, rc,
):
    s = lax.axis_index("seq")
    f = lax.axis_index("fsdp")
    z = f // 2
    c = f % 2
    length = ct_ref.shape[0]
    patches = length // STRIDE
    pr = pw_ref.shape[0]
    q = pr // n_s
    parts = D // pr
    half_rows = (D // 2) // n_s

    def copy(src, dst, send, recv, dev):
        cpy = pltpu.make_async_remote_copy(
            src_ref=src, dst_ref=dst, send_sem=send, recv_sem=recv, device_id=dev, device_id_type=MESH
        )
        cpy.start()

    def drain(ref, sem):
        pltpu.make_async_copy(ref, ref, sem).wait()

    partner = (s, 2 * z + 1 - c)
    mypart = pl.ds(pl.multiple_of(c * patches, patches), patches)

    def zdev(i):
        zi = lax.rem(z + i, n_z)
        return zi, (s, 2 * zi + c)

    def sdev(i):
        si = lax.rem(s + i, n_s)
        return si, (si, f)

    own_panel = pltpu.make_async_copy(pw_ref, w.at[f], sem_l.at[0])
    own_panel.start()

    barrier = pltpu.get_barrier_semaphore()
    pl.semaphore_signal(barrier, inc=1, device_id=partner, device_id_type=MESH)
    for i in range(1, n_z):
        pl.semaphore_signal(barrier, inc=1, device_id=zdev(i)[1], device_id_type=MESH)
    for i in range(1, n_s):
        pl.semaphore_signal(barrier, inc=1, device_id=sdev(i)[1], device_id_type=MESH)
    pl.semaphore_wait(barrier, 1 + (n_z - 1) + (n_s - 1))

    for i in range(1, n_z):
        _, dev = zdev(n_z - i)
        copy(pw_ref.at[pl.ds(pl.multiple_of(s * q, q), q)],
             w.at[f, pl.ds(pl.multiple_of(s * q, q), q)], s1.at[i], r1.at[z], dev)
    copy(pw_ref, w.at[f], s3.at[z], r3.at[z], partner)

    @pl.when(s > 0)
    def _():
        dev = (s - 1, f)
        copy(x_ref.at[pl.ds(0, 16)], hx, sem_h.at[0], sem_h.at[1], dev)
        copy(ct_ref.at[pl.ds(0, 16)], hc, sem_h.at[2], sem_h.at[3], dev)
        copy(doc_ref.at[:, pl.ds(0, 128)], hd, sem_h.at[4], sem_h.at[5], dev)

    for lb in range(4):
        xf[lb, pl.ds(0, length)] = x_ref[:, lb * 128:(lb + 1) * 128].astype(F32)
        cf[lb, pl.ds(0, length)] = ct_ref[:, lb * 128:(lb + 1) * 128].astype(F32)
    df[pl.ds(0, length)] = jnp.transpose(
        jnp.broadcast_to(doc_ref[...].astype(F32), (128, length)), (1, 0)
    )

    for ch in range(CG):
        block = cw_ref[:, ch].astype(F32).reshape(KERNEL * CG, GROUPS)
        pacc[pl.ds(ch, GROUPS, stride=CG), :] = jnp.transpose(block, (1, 0))
    lane_of = lax.broadcasted_iota(jnp.int32, (128, 256), 0)
    want = lax.broadcasted_iota(jnp.int32, (128, 256), 1) % CG
    diag = (
        lax.broadcasted_iota(jnp.int32, (256, 256), 0) // CG
        == lax.broadcasted_iota(jnp.int32, (256, 256), 1) // CG
    )

    def build(kb, carry):
        k = kb // 2
        spread = (lane_of == k * CG + want).astype(F32).astype(BF)
        piece = pacc[pl.ds(pl.multiple_of((kb % 2) * 256, 256), 256), :].astype(BF)
        wd[kb] = jnp.where(diag, dot(piece, spread, 1, 0), 0.0).astype(BF)
        return carry

    lax.fori_loop(0, 2 * KERNEL, build, 0)

    @pl.when(s == n_s - 1)
    def _():
        xf[:, pl.ds(length, 8)] = jnp.zeros((4, 8, 128), F32)
        cf[:, pl.ds(length, 8)] = jnp.zeros((4, 8, 128), F32)
        df[pl.ds(length, 8)] = jnp.full((8, 128), -1.0, F32)

    @pl.when(s < n_s - 1)
    def _():
        drain(hx, sem_h.at[1])
        drain(hc, sem_h.at[3])
        drain(hd, sem_h.at[5])
        top = hx[...].astype(F32)
        topc = hc[...].astype(F32)
        for lb in range(4):
            xf[lb, pl.ds(length, 8)] = top[:8, lb * 128:(lb + 1) * 128]
            cf[lb, pl.ds(length, 8)] = topc[:8, lb * 128:(lb + 1) * 128]
        df[pl.ds(length, 8)] = jnp.transpose(
            jnp.broadcast_to(hd[...].astype(F32), (128, 128)), (1, 0)
        )[:8]

    @pl.when(s > 0)
    def _():
        drain(hx, sem_h.at[0])
        drain(hc, sem_h.at[2])
        drain(hd, sem_h.at[4])

    def taps(ref, k):
        return jnp.concatenate(
            [ref[lb, pl.ds(k, patches, stride=STRIDE), :] for lb in range(4)], axis=1
        )

    first_doc = df[pl.ds(0, patches, stride=STRIDE), :]
    for k in range(KERNEL):
        keep = (df[pl.ds(k, patches, stride=STRIDE), :] == first_doc).astype(F32)
        kp[k] = keep
        kw = wide(keep)
        win[k] = (taps(xf, k) * kw).astype(BF)
        upk = (taps(cf, k) * kw).astype(BF)
        for part in range(parts):
            up[k * parts + part] = upk[:, part * pr:(part + 1) * pr]

    shape = (pr, D)
    flat = (f * pr + lax.broadcasted_iota(jnp.int32, shape, 0)) * jnp.int32(D) + lax.broadcasted_iota(
        jnp.int32, shape, 1
    )
    dith[...] = QUANT * (mix_bits(flat, seed_ref[0], step_ref[0]) - 0.5)

    hid[...] = jnp.zeros_like(hid)

    def conv(k, carry):
        for b in range(2):
            hid[:, b * 256:(b + 1) * 256] += dot(win[k, :, b * 256:(b + 1) * 256], wd[2 * k + b], 1, 0)
        return carry

    lax.fori_loop(0, KERNEL, conv, 0)
    def forward(i, carry):
        zi = lax.rem(z + i, n_z)
        fi = 2 * zi + c
        piece = w.at[fi, pl.ds(pl.multiple_of(s * q, q), q)]
        drain(piece, r1.at[zi])
        for j in range(1, n_s):
            _, dev = sdev(j)
            copy(piece, piece, s2.at[zi], r2.at[zi], dev)
        return carry

    lax.fori_loop(1, n_z, forward, 0)

    hidden = hid[...]
    factor = lax.rsqrt(jnp.mean(hidden * hidden, axis=-1, keepdims=True) + 1e-06)
    fac[...] = jnp.broadcast_to(factor, (patches, 128))
    norm[mypart] = (hidden * factor * gain_ref[...]).astype(BF)
    copy(norm.at[mypart], norm.at[mypart], sn.at[0], sn.at[1], partner)
    gn[...] = jnp.zeros_like(gn)
    own_panel.wait()

    def panel(fi, dst):
        pre = dot(norm[mypart], w[fi], 1, 1)
        g = (up[fi].astype(F32) * gelu_grad(pre)).astype(BF)
        dst[...] = g
        gn[...] += dot(g, w[fi], 1, 0)

    def sums(zi):
        drain(gps.at[0], rg.at[zi])
        total = dot(gpo[zi], norm[...], 0, 0)
        sf[...] = total
        ps[zi] = total.astype(BF)
        own[zi] = sf[pl.ds(pl.multiple_of(s * q, q), q), :]
        for j in range(1, n_s):
            sj, dev = sdev(j)
            copy(ps.at[zi, pl.ds(pl.multiple_of(sj * q, q), q)], rs1.at[zi, s], ss.at[zi], rs.at[zi], dev)

    def step(i, carry):
        zi = lax.rem(z + i, n_z)

        @pl.when(i > 0)
        def _():
            drain(w.at[0, pl.ds(0, (n_s - 1) * q)], r2.at[zi])
            copy(w.at[2 * zi + c], w.at[2 * zi + c], s3.at[zi], r3.at[zi], partner)

        panel(2 * zi + c, gpo.at[zi, mypart])
        drain(w.at[0], r3.at[zi])
        panel(2 * zi + 1 - c, gps.at[zi])
        copy(gps.at[zi], gpo.at[zi, mypart], sg.at[zi], rg.at[zi], partner)

        @pl.when(i == 0)
        def _():
            drain(gh, sn.at[1])

        @pl.when(i > 0)
        def _():
            sums(lax.rem(z + i - 1, n_z))

        return carry

    lax.fori_loop(0, n_z, step, 0)
    sums(lax.rem(z + n_z - 1, n_z))

    hidden = hid[...]
    factor = fac[:, :1]
    grad_norm = gn[...]
    gain_part = jnp.sum(grad_norm * hidden * factor, axis=0, keepdims=True)
    gained = gain_ref[...] * grad_norm
    gh[...] = (
        factor * gained
        - hidden * (factor * factor * factor) * jnp.mean(gained * hidden, axis=-1, keepdims=True)
    ).astype(BF)

    def upper(t):
        return wide(kp[STRIDE + t]) * jnp.concatenate(
            [dot(gh[:, b * 256:(b + 1) * 256], wd[2 * (STRIDE + t) + b], 1, 1) for b in range(2)], axis=1
        )

    cols = lax.broadcasted_iota(jnp.int32, (128, 128), 1) // CG
    small = lax.broadcasted_iota(jnp.int32, (128, 128), 0) // CG == cols
    pacc[...] = jnp.zeros_like(pacc)

    def conv_back(k, carry):
        for b in range(4):
            lanes = slice(b * 128, (b + 1) * 128)
            full = jnp.where(small, dot(jnp.transpose(win[k, :, lanes], (1, 0)), gh[:, lanes], 1, 0), 0.0)
            full = full + pltpu.roll(full, 64, 1)
            full = full + pltpu.roll(full, 32, 1)
            full = full + pltpu.roll(full, 16, 1)
            pacc[lanes, :] = jnp.where(cols == k, full, pacc[lanes, :])
        return carry

    [conv_back(k, 0) for k in range(KERNEL)]
    cp[...] = jnp.zeros_like(cp)
    cp[:, :, pl.ds(0, half_rows), :] = pacc[...].reshape(2, n_s, half_rows, 128)
    for b in range(4):
        cp[0, 0, pl.ds(half_rows + b, 1), :] = gain_part[:, b * 128:(b + 1) * 128]
    copy(cp.at[1 - c], cpx, sc.at[0], rc.at[0], partner)

    def reduce_seq(i, carry):
        zi = lax.rem(z + i, n_z)
        drain(rs1.at[0, pl.ds(0, n_s - 1)], rs.at[zi])
        total = own[zi]
        for j in range(1, n_s):
            total = total + rs1[zi, sdev(j)[0]].astype(F32)

        @pl.when(i > 0)
        def _():
            zs[i] = total.astype(BF)
            copy(zs.at[i], rs2.at[z], sz.at[i], rz.at[i], (s, 2 * zi + c))

        @pl.when(i == 0)
        def _():
            own[z] = total

        return carry

    lax.fori_loop(0, n_z - 1, reduce_seq, 0)

    for t in range(STRIDE):
        tail = gh[pl.ds(patches - 16, 16), :]
        edge = jnp.concatenate(
            [dot(tail[:, b * 256:(b + 1) * 256], wd[2 * (STRIDE + t) + b], 1, 1) for b in range(2)], axis=1
        )
        hsend[pl.ds(t, 1), :] = edge[15:, :] * wide(kp[STRIDE + t, pl.ds(patches - 1, 1), :])

    @pl.when(s < n_s - 1)
    def _():
        copy(hsend, hrecv, sem_h.at[6], sem_h.at[7], (s + 1, f))

    drain(cpx, rc.at[0])
    c1[...] = cp[c] + cpx[...]
    for j in range(1, n_s):
        sj, dev = sdev(j)
        copy(c1.at[sj], c2.at[s], sc.at[1], rc.at[1], dev)

    lax.fori_loop(n_z - 1, n_z, reduce_seq, 0)

    drain(c2.at[pl.ds(0, n_s - 1)], rc.at[1])
    total = c1[s]
    for j in range(1, n_s):
        total = total + c2[sdev(j)[0]]
    c3[z] = total
    for i in range(1, n_z):
        copy(c3.at[z], c3.at[z], sc.at[2], rc.at[2], zdev(i)[1])

    total = own[z]
    for i in range(1, n_z):
        drain(rs2.at[0], rz.at[i])
        total = total + rs2[zdev(n_z - i)[0]].astype(F32)
    mine = pl.ds(pl.multiple_of(s * q, q), q)
    fin[mine] = total.astype(BF)
    for j in range(1, n_s):
        copy(fin.at[mine], fin.at[mine], sf_s.at[0], sf_r.at[0], sdev(j)[1])

    drain(c3.at[pl.ds(0, n_z - 1)], rc.at[2])
    total = c3[0]
    for i in range(1, n_z):
        total = total + c3[i]
    c4[s] = total
    for j in range(1, n_s):
        copy(c4.at[s], c4.at[s], sc.at[3], rc.at[3], sdev(j)[1])

    row = lax.broadcasted_iota(jnp.int32, (patches, D), 0)
    for t in range(STRIDE):
        hi = upper(t)
        lo = wide(kp[t]) * jnp.concatenate(
            [dot(gh[:, b * 256:(b + 1) * 256], wd[2 * t + b], 1, 1) for b in range(2)], axis=1
        )
        value = taps(cf, t) + lo + jnp.where(row == 0, 0.0, pltpu.roll(hi, 1, 0))
        for lb in range(4):
            xf[lb, pl.ds(t, patches, stride=STRIDE), :] = value[:, lb * 128:(lb + 1) * 128]

    for lb in range(4):
        gb_ref[:, lb * 128:(lb + 1) * 128] = xf[lb, pl.ds(0, length)]

    drain(c4.at[pl.ds(0, n_s - 1)], rc.at[3])
    copy(c4, c5, sc.at[4], rc.at[4], partner)

    @pl.when(s > 0)
    def _():
        drain(hrecv, sem_h.at[7])
        gb_ref[pl.ds(0, 8), :] += jnp.where(
            lax.broadcasted_iota(jnp.int32, (8, D), 0) < STRIDE, hrecv[...], 0.0
        )

    @pl.when(s < n_s - 1)
    def _():
        drain(hsend, sem_h.at[6])

    co_ref[c] = c4[...] * scale
    drain(c5, rc.at[4])
    co_ref[1 - c] = c5[...] * scale
    for h in range(2):
        for j in range(n_s):
            pacc[pl.ds((h * n_s + j) * half_rows, half_rows), :] = co_ref[h, j, pl.ds(0, half_rows), :]
    for ch in range(CG):
        block = jnp.transpose(pacc[pl.ds(ch, GROUPS, stride=CG), :], (1, 0))
        conv_ref[:, ch] = block.reshape(KERNEL, CG, GROUPS)
    for b in range(4):
        go_ref[:, b * 128:(b + 1) * 128] = co_ref[0, 0, pl.ds(half_rows + b, 1), :]

    drain(fin.at[pl.ds(0, (n_s - 1) * q)], sf_r.at[0])
    gpo_ref[...] = fin[...].astype(F32) * scale + dith[...]

    for i in range(1, n_z):
        drain(w.at[0, pl.ds(0, q)], s1.at[i])
        drain(zs.at[0], sz.at[i])
        zi, _ = zdev(i)
        drain(w.at[0, pl.ds(0, (n_s - 1) * q)], s2.at[zi])
    for i in range(n_z):
        drain(w.at[0], s3.at[i])
        drain(gps.at[0], sg.at[i])
        drain(rs1.at[0, pl.ds(0, n_s - 1)], ss.at[i])
    drain(gh, sn.at[0])
    drain(cpx, sc.at[0])
    drain(c2.at[pl.ds(0, n_s - 1)], sc.at[1])
    drain(c3.at[pl.ds(0, n_z - 1)], sc.at[2])
    drain(c4.at[pl.ds(0, n_s - 1)], sc.at[3])
    drain(c4, sc.at[4])
    drain(fin.at[pl.ds(0, (n_s - 1) * q)], sf_s.at[0])


def per_device(
    n_s, n_f, byte_rows, cotangent, doc_ids, conv_weight, norm_gain, proj_weight, round_seed, step_count
):
    length = byte_rows.shape[1]
    patches = length // STRIDE
    pr = proj_weight.shape[0]
    n_z = n_f // 2
    q = pr // n_s
    rows = (D // 2) // n_s + 8
    scale = 1.0 / math.sqrt(patches * n_s * n_f)
    v = pltpu.VMEM
    dma = pltpu.SemaphoreType.DMA
    vm = pl.BlockSpec(memory_space=pltpu.VMEM)
    smem = pl.BlockSpec(memory_space=pltpu.SMEM)
    scratch = [
        v((2, n_s, rows, 128), F32),
        v((4, length + 8, 128), F32), v((4, length + 8, 128), F32), v((length + 8, 128), F32),
        v((16, D), BF), v((16, D), BF), v((1, 128), jnp.int32),
        v((KERNEL, patches, D), BF), v((n_f, patches, pr), BF), v((KERNEL, patches, 128), F32),
        v((2 * KERNEL, 256, 256), BF), v((n_f, pr, D), BF),
        v((n_z, 2 * patches, pr), BF), v((n_z, patches, pr), BF),
        v((n_z, pr, D), BF), v((n_z, n_s, q, D), BF), v((pr, D), F32), v((n_z, q, D), F32),
        v((n_z, q, D), BF), v((n_z, q, D), BF), v((pr, D), BF), v((pr, D), F32),
        v((patches, D), F32), v((patches, D), F32), v((patches, 128), F32),
        v((2 * patches, D), BF), v((patches, D), BF),
        v((8, D), F32), v((8, D), F32),
        v((D, 128), F32), v((2, n_s, rows, 128), F32), v((n_s, rows, 128), F32),
        v((n_s, rows, 128), F32), v((n_s, rows, 128), F32), v((n_z, rows, 128), F32),
        v((n_s, rows, 128), F32), v((n_s, rows, 128), F32),
        dma((1,)), dma((8,)), dma((n_z,)), dma((n_z,)), dma((n_z,)), dma((n_z,)), dma((n_z,)), dma((n_z,)),
        dma((n_z,)), dma((n_z,)), dma((2,)), dma((n_z,)), dma((n_z,)), dma((n_z,)), dma((n_z,)),
        dma((1,)), dma((1,)), dma((5,)), dma((5,)),
    ]
    grad_bytes, grad_proj, grad_conv, grad_gain = pl.pallas_call(
        functools.partial(kernel, n_s, n_z, scale),
        out_shape=(
            jax.ShapeDtypeStruct((length, D), F32),
            jax.ShapeDtypeStruct((pr, D), F32),
            jax.ShapeDtypeStruct((KERNEL, CG, CG, GROUPS), F32),
            jax.ShapeDtypeStruct((1, D), F32),
        ),
        in_specs=[vm, vm, vm, vm, vm, pl.BlockSpec(memory_space=pl.ANY), smem, smem],
        out_specs=(vm, vm, vm, vm),
        scratch_shapes=scratch,
        compiler_params=pltpu.CompilerParams(
            collective_id=0, has_side_effects=True, vmem_limit_bytes=58 * 1024 * 1024
        ),
    )(
        byte_rows[0], cotangent[0], doc_ids, conv_weight.transpose(0, 2, 3, 1), norm_gain[None],
        proj_weight, round_seed, step_count,
    )
    return grad_bytes[None], grad_proj, grad_conv.transpose(0, 3, 1, 2), grad_gain[0]


def solution(mesh):
    in_specs = (
        P("fsdp", "seq", None),
        P("fsdp", "seq", None),
        P("fsdp", "seq"),
        P(),
        P(),
        P("fsdp", None),
        P(),
        P(),
    )
    out_specs = (P("fsdp", "seq", None), P("fsdp", None), P(), P())
    return jax.shard_map(
        functools.partial(per_device, mesh.shape["seq"], mesh.shape["fsdp"]),
        mesh=mesh, in_specs=in_specs, out_specs=out_specs, check_vma=False,
    )
```

```python
import functools
import math

import jax
import jax.numpy as jnp
from jax import lax
from jax.experimental import pallas as pl
from jax.experimental.pallas import tpu as pltpu
from jax.sharding import PartitionSpec as P

GROUPS = 32
KERNEL = 8
STRIDE = 4
CG = 16
D = GROUPS * CG

GELU_A = 0.7978845608028654
GELU_B = 0.044715
QUANT = 0.25

MESH = pl.DeviceIdType.MESH
BF = jnp.bfloat16
F32 = jnp.float32


def gelu_grad(values):
    tangent = jnp.tanh(GELU_A * (values + GELU_B * values * values * values))
    return 0.5 * (1.0 + tangent) + 0.5 * values * (1.0 - tangent * tangent) * GELU_A * (
        1.0 + 3.0 * GELU_B * values * values
    )


def mix_bits(flat_index, seed_value, step_value):
    hashed = (
        flat_index * jnp.int32(-1640531535)
        + seed_value * jnp.int32(-2048144777)
        + step_value * jnp.int32(-1028477379)
    )
    hashed = hashed ^ lax.shift_right_logical(hashed, jnp.int32(16))
    hashed = hashed * jnp.int32(2146121005)
    hashed = hashed ^ lax.shift_right_logical(hashed, jnp.int32(15))
    hashed = hashed * jnp.int32(-2073254261)
    hashed = hashed ^ lax.shift_right_logical(hashed, jnp.int32(16))
    return lax.shift_right_logical(hashed, jnp.int32(8)).astype(F32) / 16777216.0


def dot(a, b, ca, cb):
    return lax.dot_general(a, b, (((ca,), (cb,)), ((), ())), preferred_element_type=F32)


def wide(mask):
    return jnp.concatenate([mask] * (D // 128), axis=1)


def kernel(
    n_s, n_z, scale,
    x_ref, ct_ref, doc_ref, cw_ref, gain_ref, pw_ref, seed_ref, step_ref,
    gb_ref, gpo_ref, conv_ref, go_ref,
    co_ref, xf, cf, df, hx, hc, hd, win, up, kp, wd, w, gpo, gps, ps, rs1, sf, own, rs2, zs, fin, dith,
    gn, hid, fac, norm, gh, hsend, hrecv,
    pacc, cp, cpx, c1, c2, c3, c4, c5,
    sem_l, sem_h, s1, r1, s2, r2, s3, r3, sg, rg, sn, ss, rs, sz, rz, sf_s, sf_r, sc, rc,
):
    s = lax.axis_index("seq")
    f = lax.axis_index("fsdp")
    z = f // 2
    c = f % 2
    length = ct_ref.shape[0]
    patches = length // STRIDE
    pr = pw_ref.shape[0]
    q = pr // n_s
    parts = D // pr
    half_rows = (D // 2) // n_s

    def copy(src, dst, send, recv, dev):
        cpy = pltpu.make_async_remote_copy(
            src_ref=src, dst_ref=dst, send_sem=send, recv_sem=recv, device_id=dev, device_id_type=MESH
        )
        cpy.start()

    def drain(ref, sem):
        pltpu.make_async_copy(ref, ref, sem).wait()

    partner = (s, 2 * z + 1 - c)
    mypart = pl.ds(pl.multiple_of(c * patches, patches), patches)

    def zdev(i):
        zi = lax.rem(z + i, n_z)
        return zi, (s, 2 * zi + c)

    def sdev(i):
        si = lax.rem(s + i, n_s)
        return si, (si, f)

    own_panel = pltpu.make_async_copy(pw_ref, w.at[f], sem_l.at[0])
    own_panel.start()

    barrier = pltpu.get_barrier_semaphore()
    pl.semaphore_signal(barrier, inc=1, device_id=partner, device_id_type=MESH)
    for i in range(1, n_z):
        pl.semaphore_signal(barrier, inc=1, device_id=zdev(i)[1], device_id_type=MESH)
    for i in range(1, n_s):
        pl.semaphore_signal(barrier, inc=1, device_id=sdev(i)[1], device_id_type=MESH)
    pl.semaphore_wait(barrier, 1 + (n_z - 1) + (n_s - 1))

    for i in range(1, n_z):
        _, dev = zdev(n_z - i)
        copy(pw_ref.at[pl.ds(pl.multiple_of(s * q, q), q)],
             w.at[f, pl.ds(pl.multiple_of(s * q, q), q)], s1.at[i], r1.at[z], dev)
    copy(pw_ref, w.at[f], s3.at[z], r3.at[z], partner)

    @pl.when(s > 0)
    def _():
        dev = (s - 1, f)
        copy(x_ref.at[pl.ds(0, 16)], hx, sem_h.at[0], sem_h.at[1], dev)
        copy(ct_ref.at[pl.ds(0, 16)], hc, sem_h.at[2], sem_h.at[3], dev)
        copy(doc_ref.at[:, pl.ds(0, 128)], hd, sem_h.at[4], sem_h.at[5], dev)

    for lb in range(4):
        xf[lb, pl.ds(0, length)] = x_ref[:, lb * 128:(lb + 1) * 128].astype(F32)
        cf[lb, pl.ds(0, length)] = ct_ref[:, lb * 128:(lb + 1) * 128].astype(F32)
    df[pl.ds(0, length)] = jnp.transpose(
        jnp.broadcast_to(doc_ref[...].astype(F32), (128, length)), (1, 0)
    )

    for ch in range(CG):
        block = cw_ref[:, ch].astype(F32).reshape(KERNEL * CG, GROUPS)
        pacc[pl.ds(ch, GROUPS, stride=CG), :] = jnp.transpose(block, (1, 0))
    lane_of = lax.broadcasted_iota(jnp.int32, (128, 256), 0)
    want = lax.broadcasted_iota(jnp.int32, (128, 256), 1) % CG
    diag = (
        lax.broadcasted_iota(jnp.int32, (256, 256), 0) // CG
        == lax.broadcasted_iota(jnp.int32, (256, 256), 1) // CG
    )

    def build(kb, carry):
        k = kb // 2
        spread = (lane_of == k * CG + want).astype(F32).astype(BF)
        piece = pacc[pl.ds(pl.multiple_of((kb % 2) * 256, 256), 256), :].astype(BF)
        wd[kb] = jnp.where(diag, dot(piece, spread, 1, 0), 0.0).astype(BF)
        return carry

    lax.fori_loop(0, 2 * KERNEL, build, 0)

    @pl.when(s == n_s - 1)
    def _():
        xf[:, pl.ds(length, 8)] = jnp.zeros((4, 8, 128), F32)
        cf[:, pl.ds(length, 8)] = jnp.zeros((4, 8, 128), F32)
        df[pl.ds(length, 8)] = jnp.full((8, 128), -1.0, F32)

    @pl.when(s < n_s - 1)
    def _():
        drain(hx, sem_h.at[1])
        drain(hc, sem_h.at[3])
        drain(hd, sem_h.at[5])
        top = hx[...].astype(F32)
        topc = hc[...].astype(F32)
        for lb in range(4):
            xf[lb, pl.ds(length, 8)] = top[:8, lb * 128:(lb + 1) * 128]
            cf[lb, pl.ds(length, 8)] = topc[:8, lb * 128:(lb + 1) * 128]
        df[pl.ds(length, 8)] = jnp.transpose(
            jnp.broadcast_to(hd[...].astype(F32), (128, 128)), (1, 0)
        )[:8]

    @pl.when(s > 0)
    def _():
        drain(hx, sem_h.at[0])
        drain(hc, sem_h.at[2])
        drain(hd, sem_h.at[4])

    def taps(ref, k):
        return jnp.concatenate(
            [ref[lb, pl.ds(k, patches, stride=STRIDE), :] for lb in range(4)], axis=1
        )

    first_doc = df[pl.ds(0, patches, stride=STRIDE), :]
    for k in range(KERNEL):
        keep = (df[pl.ds(k, patches, stride=STRIDE), :] == first_doc).astype(F32)
        kp[k] = keep
        kw = wide(keep)
        win[k] = (taps(xf, k) * kw).astype(BF)
        upk = (taps(cf, k) * kw).astype(BF)
        for part in range(parts):
            up[k * parts + part] = upk[:, part * pr:(part + 1) * pr]

    shape = (pr, D)
    flat = (f * pr + lax.broadcasted_iota(jnp.int32, shape, 0)) * jnp.int32(D) + lax.broadcasted_iota(
        jnp.int32, shape, 1
    )
    dith[...] = QUANT * (mix_bits(flat, seed_ref[0], step_ref[0]) - 0.5)

    def forward(i, carry):
        zi = lax.rem(z + i, n_z)
        fi = 2 * zi + c
        piece = w.at[fi, pl.ds(pl.multiple_of(s * q, q), q)]
        drain(piece, r1.at[zi])
        for j in range(1, n_s):
            _, dev = sdev(j)
            copy(piece, piece, s2.at[zi], r2.at[zi], dev)
        return carry

    lax.fori_loop(1, n_z, forward, 0)

    hid[...] = jnp.zeros_like(hid)

    def conv(k, carry):
        for b in range(2):
            hid[:, b * 256:(b + 1) * 256] += dot(win[k, :, b * 256:(b + 1) * 256], wd[2 * k + b], 1, 0)
        return carry

    lax.fori_loop(0, KERNEL, conv, 0)

    hidden = hid[...]
    factor = lax.rsqrt(jnp.mean(hidden * hidden, axis=-1, keepdims=True) + 1e-06)
    fac[...] = jnp.broadcast_to(factor, (patches, 128))
    norm[mypart] = (hidden * factor * gain_ref[...]).astype(BF)
    copy(norm.at[mypart], norm.at[mypart], sn.at[0], sn.at[1], partner)
    gn[...] = jnp.zeros_like(gn)
    own_panel.wait()

    def panel(fi, dst):
        pre = dot(norm[mypart], w[fi], 1, 1)
        g = (up[fi].astype(F32) * gelu_grad(pre)).astype(BF)
        dst[...] = g
        gn[...] += dot(g, w[fi], 1, 0)

    def sums(zi):
        drain(gps.at[0], rg.at[zi])
        total = dot(gpo[zi], norm[...], 0, 0)
        sf[...] = total
        ps[zi] = total.astype(BF)
        own[zi] = sf[pl.ds(pl.multiple_of(s * q, q), q), :]
        for j in range(1, n_s):
            sj, dev = sdev(j)
            copy(ps.at[zi, pl.ds(pl.multiple_of(sj * q, q), q)], rs1.at[zi, s], ss.at[zi], rs.at[zi], dev)

    def step(i, carry):
        zi = lax.rem(z + i, n_z)

        @pl.when(i > 0)
        def _():
            drain(w.at[0, pl.ds(0, (n_s - 1) * q)], r2.at[zi])
            copy(w.at[2 * zi + c], w.at[2 * zi + c], s3.at[zi], r3.at[zi], partner)

        panel(2 * zi + c, gpo.at[zi, mypart])
        drain(w.at[0], r3.at[zi])
        panel(2 * zi + 1 - c, gps.at[zi])
        copy(gps.at[zi], gpo.at[zi, mypart], sg.at[zi], rg.at[zi], partner)

        @pl.when(i == 0)
        def _():
            drain(gh, sn.at[1])

        @pl.when(i > 0)
        def _():
            sums(lax.rem(z + i - 1, n_z))

        return carry

    lax.fori_loop(0, n_z, step, 0)
    sums(lax.rem(z + n_z - 1, n_z))

    hidden = hid[...]
    factor = fac[:, :1]
    grad_norm = gn[...]
    gain_part = jnp.sum(grad_norm * hidden * factor, axis=0, keepdims=True)
    gained = gain_ref[...] * grad_norm
    gh[...] = (
        factor * gained
        - hidden * (factor * factor * factor) * jnp.mean(gained * hidden, axis=-1, keepdims=True)
    ).astype(BF)

    def upper(t):
        return wide(kp[STRIDE + t]) * jnp.concatenate(
            [dot(gh[:, b * 256:(b + 1) * 256], wd[2 * (STRIDE + t) + b], 1, 1) for b in range(2)], axis=1
        )

    cols = lax.broadcasted_iota(jnp.int32, (128, 128), 1) // CG
    small = lax.broadcasted_iota(jnp.int32, (128, 128), 0) // CG == cols
    pacc[...] = jnp.zeros_like(pacc)

    def conv_back(k, carry):
        for b in range(4):
            lanes = slice(b * 128, (b + 1) * 128)
            full = jnp.where(small, dot(jnp.transpose(win[k, :, lanes], (1, 0)), gh[:, lanes], 1, 0), 0.0)
            full = full + pltpu.roll(full, 64, 1)
            full = full + pltpu.roll(full, 32, 1)
            full = full + pltpu.roll(full, 16, 1)
            pacc[lanes, :] = jnp.where(cols == k, full, pacc[lanes, :])
        return carry

    [conv_back(k, 0) for k in range(KERNEL)]
    cp[...] = jnp.zeros_like(cp)
    cp[:, :, pl.ds(0, half_rows), :] = pacc[...].reshape(2, n_s, half_rows, 128)
    for b in range(4):
        cp[0, 0, pl.ds(half_rows + b, 1), :] = gain_part[:, b * 128:(b + 1) * 128]
    copy(cp.at[1 - c], cpx, sc.at[0], rc.at[0], partner)

    def reduce_seq(i, carry):
        zi = lax.rem(z + i, n_z)
        drain(rs1.at[0, pl.ds(0, n_s - 1)], rs.at[zi])
        total = own[zi]
        for j in range(1, n_s):
            total = total + rs1[zi, sdev(j)[0]].astype(F32)

        @pl.when(i > 0)
        def _():
            zs[i] = total.astype(BF)
            copy(zs.at[i], rs2.at[z], sz.at[i], rz.at[i], (s, 2 * zi + c))

        @pl.when(i == 0)
        def _():
            own[z] = total

        return carry

    lax.fori_loop(0, n_z - 1, reduce_seq, 0)

    for t in range(STRIDE):
        tail = gh[pl.ds(patches - 16, 16), :]
        edge = jnp.concatenate(
            [dot(tail[:, b * 256:(b + 1) * 256], wd[2 * (STRIDE + t) + b], 1, 1) for b in range(2)], axis=1
        )
        hsend[pl.ds(t, 1), :] = edge[15:, :] * wide(kp[STRIDE + t, pl.ds(patches - 1, 1), :])

    @pl.when(s < n_s - 1)
    def _():
        copy(hsend, hrecv, sem_h.at[6], sem_h.at[7], (s + 1, f))

    drain(cpx, rc.at[0])
    c1[...] = cp[c] + cpx[...]
    for j in range(1, n_s):
        sj, dev = sdev(j)
        copy(c1.at[sj], c2.at[s], sc.at[1], rc.at[1], dev)

    lax.fori_loop(n_z - 1, n_z, reduce_seq, 0)

    drain(c2.at[pl.ds(0, n_s - 1)], rc.at[1])
    total = c1[s]
    for j in range(1, n_s):
        total = total + c2[sdev(j)[0]]
    c3[z] = total
    for i in range(1, n_z):
        copy(c3.at[z], c3.at[z], sc.at[2], rc.at[2], zdev(i)[1])

    total = own[z]
    for i in range(1, n_z):
        drain(rs2.at[0], rz.at[i])
        total = total + rs2[zdev(n_z - i)[0]].astype(F32)
    mine = pl.ds(pl.multiple_of(s * q, q), q)
    fin[mine] = total.astype(BF)
    for j in range(1, n_s):
        copy(fin.at[mine], fin.at[mine], sf_s.at[0], sf_r.at[0], sdev(j)[1])

    drain(c3.at[pl.ds(0, n_z - 1)], rc.at[2])
    total = c3[0]
    for i in range(1, n_z):
        total = total + c3[i]
    c4[s] = total
    for j in range(1, n_s):
        copy(c4.at[s], c4.at[s], sc.at[3], rc.at[3], sdev(j)[1])

    row = lax.broadcasted_iota(jnp.int32, (patches, D), 0)
    for t in range(STRIDE):
        hi = upper(t)
        lo = wide(kp[t]) * jnp.concatenate(
            [dot(gh[:, b * 256:(b + 1) * 256], wd[2 * t + b], 1, 1) for b in range(2)], axis=1
        )
        value = taps(cf, t) + lo + jnp.where(row == 0, 0.0, pltpu.roll(hi, 1, 0))
        for lb in range(4):
            xf[lb, pl.ds(t, patches, stride=STRIDE), :] = value[:, lb * 128:(lb + 1) * 128]

    for lb in range(4):
        gb_ref[:, lb * 128:(lb + 1) * 128] = xf[lb, pl.ds(0, length)]

    drain(c4.at[pl.ds(0, n_s - 1)], rc.at[3])
    copy(c4, c5, sc.at[4], rc.at[4], partner)

    @pl.when(s > 0)
    def _():
        drain(hrecv, sem_h.at[7])
        gb_ref[pl.ds(0, 8), :] += jnp.where(
            lax.broadcasted_iota(jnp.int32, (8, D), 0) < STRIDE, hrecv[...], 0.0
        )

    @pl.when(s < n_s - 1)
    def _():
        drain(hsend, sem_h.at[6])

    co_ref[c] = c4[...] * scale
    drain(c5, rc.at[4])
    co_ref[1 - c] = c5[...] * scale
    for h in range(2):
        for j in range(n_s):
            pacc[pl.ds((h * n_s + j) * half_rows, half_rows), :] = co_ref[h, j, pl.ds(0, half_rows), :]
    for ch in range(CG):
        block = jnp.transpose(pacc[pl.ds(ch, GROUPS, stride=CG), :], (1, 0))
        conv_ref[:, ch] = block.reshape(KERNEL, CG, GROUPS)
    for b in range(4):
        go_ref[:, b * 128:(b + 1) * 128] = co_ref[0, 0, pl.ds(half_rows + b, 1), :]

    drain(fin.at[pl.ds(0, (n_s - 1) * q)], sf_r.at[0])
    gpo_ref[...] = fin[...].astype(F32) * scale + dith[...]

    for i in range(1, n_z):
        drain(w.at[0, pl.ds(0, q)], s1.at[i])
        drain(zs.at[0], sz.at[i])
        zi, _ = zdev(i)
        drain(w.at[0, pl.ds(0, (n_s - 1) * q)], s2.at[zi])
    for i in range(n_z):
        drain(w.at[0], s3.at[i])
        drain(gps.at[0], sg.at[i])
        drain(rs1.at[0, pl.ds(0, n_s - 1)], ss.at[i])
    drain(gh, sn.at[0])
    drain(cpx, sc.at[0])
    drain(c2.at[pl.ds(0, n_s - 1)], sc.at[1])
    drain(c3.at[pl.ds(0, n_z - 1)], sc.at[2])
    drain(c4.at[pl.ds(0, n_s - 1)], sc.at[3])
    drain(c4, sc.at[4])
    drain(fin.at[pl.ds(0, (n_s - 1) * q)], sf_s.at[0])


def per_device(
    n_s, n_f, byte_rows, cotangent, doc_ids, conv_weight, norm_gain, proj_weight, round_seed, step_count
):
    length = byte_rows.shape[1]
    patches = length // STRIDE
    pr = proj_weight.shape[0]
    n_z = n_f // 2
    q = pr // n_s
    rows = (D // 2) // n_s + 8
    scale = 1.0 / math.sqrt(patches * n_s * n_f)
    v = pltpu.VMEM
    dma = pltpu.SemaphoreType.DMA
    vm = pl.BlockSpec(memory_space=pltpu.VMEM)
    smem = pl.BlockSpec(memory_space=pltpu.SMEM)
    scratch = [
        v((2, n_s, rows, 128), F32),
        v((4, length + 8, 128), F32), v((4, length + 8, 128), F32), v((length + 8, 128), F32),
        v((16, D), BF), v((16, D), BF), v((1, 128), jnp.int32),
        v((KERNEL, patches, D), BF), v((n_f, patches, pr), BF), v((KERNEL, patches, 128), F32),
        v((2 * KERNEL, 256, 256), BF), v((n_f, pr, D), BF),
        v((n_z, 2 * patches, pr), BF), v((n_z, patches, pr), BF),
        v((n_z, pr, D), BF), v((n_z, n_s, q, D), BF), v((pr, D), F32), v((n_z, q, D), F32),
        v((n_z, q, D), BF), v((n_z, q, D), BF), v((pr, D), BF), v((pr, D), F32),
        v((patches, D), F32), v((patches, D), F32), v((patches, 128), F32),
        v((2 * patches, D), BF), v((patches, D), BF),
        v((8, D), F32), v((8, D), F32),
        v((D, 128), F32), v((2, n_s, rows, 128), F32), v((n_s, rows, 128), F32),
        v((n_s, rows, 128), F32), v((n_s, rows, 128), F32), v((n_z, rows, 128), F32),
        v((n_s, rows, 128), F32), v((n_s, rows, 128), F32),
        dma((1,)), dma((8,)), dma((n_z,)), dma((n_z,)), dma((n_z,)), dma((n_z,)), dma((n_z,)), dma((n_z,)),
        dma((n_z,)), dma((n_z,)), dma((2,)), dma((n_z,)), dma((n_z,)), dma((n_z,)), dma((n_z,)),
        dma((1,)), dma((1,)), dma((5,)), dma((5,)),
    ]
    grad_bytes, grad_proj, grad_conv, grad_gain = pl.pallas_call(
        functools.partial(kernel, n_s, n_z, scale),
        out_shape=(
            jax.ShapeDtypeStruct((length, D), F32),
            jax.ShapeDtypeStruct((pr, D), F32),
            jax.ShapeDtypeStruct((KERNEL, CG, CG, GROUPS), F32),
            jax.ShapeDtypeStruct((1, D), F32),
        ),
        in_specs=[vm, vm, vm, vm, vm, pl.BlockSpec(memory_space=pl.ANY), smem, smem],
        out_specs=(vm, vm, vm, vm),
        scratch_shapes=scratch,
        compiler_params=pltpu.CompilerParams(
            collective_id=0, has_side_effects=True, vmem_limit_bytes=58 * 1024 * 1024
        ),
    )(
        byte_rows[0], cotangent[0], doc_ids, conv_weight.transpose(0, 2, 3, 1), norm_gain[None],
        proj_weight, round_seed, step_count,
    )
    return grad_bytes[None], grad_proj, grad_conv.transpose(0, 3, 1, 2), grad_gain[0]


def solution(mesh):
    in_specs = (
        P("fsdp", "seq", None),
        P("fsdp", "seq", None),
        P("fsdp", "seq"),
        P(),
        P(),
        P("fsdp", None),
        P(),
        P(),
    )
    out_specs = (P("fsdp", "seq", None), P("fsdp", None), P(), P())
    return jax.shard_map(
        functools.partial(per_device, mesh.shape["seq"], mesh.shape["fsdp"]),
        mesh=mesh, in_specs=in_specs, out_specs=out_specs, check_vma=False,
    )
```
